32 devices in a mesh: pop: 4 (over y, x), col: 8 (over z, core).
Axes of the slice: x: 2, y: 2, z: 4, core: 2. Of those that a mesh axis runs over, the one named last changes fastest.
Arguments:
- acts: bfloat16 [64, 64, 3584], P('pop', None, 'col'), may hold values from -6 to 6
- weight: bfloat16 [3584, 18944], P('pop', 'col'), may hold values from -0.09375 to 0.09375
- input_noise_factor: bfloat16 [64, 4, 3584], P('pop'), may hold values from -1 to 1
- output_noise_factor: bfloat16 [64, 4, 18944], P('pop', None, 'col'), may hold values from -8 to 8
- ranks: int32 [64], P('pop'), may hold values from 0 to 63, each once
Outputs:
- member_out: bfloat16 [64, 64, 18944], P('pop', None, 'col')
- step_dir: float32 [3584, 18944], P('pop', 'col')
- new_weight: bfloat16 [3584, 18944], P('pop', 'col')
The draws below stay inside these ranges and needn't reach their ends.
Inputs may be any that keep to these rules, and one draw needn't show every extreme that they name: `ranks`: every member has a different rank.
All inputs are finite; a program needn't handle non-finite values.
Results may differ from the reference program's by a relative error of at most 0.0034.
Values may be sent and summed in bfloat16 or wider, within the bound.
No kernel may reach another device: no remote copies, remote signals or barrier semaphores. Data moves between devices by JAX's collectives and lax.ppermute only.
A program may use at most 192 MiB of HBM per device.

```python
import jax
import jax.numpy as jnp
from jax import lax

D = 3584
F = 18944
RANK = 4
TOK = 64
POPULATION_SIZE = 64


def shared_signs(key):
    coin_flips = jax.random.randint(jax.random.fold_in(key, 7), (POPULATION_SIZE, RANK, 1), 0, 2)
    return (2 * coin_flips - 1).astype(jnp.float32)


def draw_input_noise_factor(key, part):
    sign_table = shared_signs(key)
    shape = (POPULATION_SIZE, RANK, D)
    fresh_part = jnp.clip(jax.random.normal(jax.random.fold_in(key, 1), shape, jnp.float32), -4.0, 4.0)
    amount = 0.6
    common = jnp.clip(jax.random.normal(jax.random.fold_in(key, 11), (D,), jnp.float32), -4.0, 4.0)
    values = (fresh_part + amount * sign_table * common[None, None, :]) * D ** (-0.5)
    return values.astype(jnp.bfloat16)


def draw_output_noise_factor(key, part):
    sign_table = shared_signs(key)
    shape = (POPULATION_SIZE, RANK, F)
    fresh_part = jnp.clip(jax.random.normal(jax.random.fold_in(key, 2), shape, jnp.float32), -4.0, 4.0)
    amount = 0.6
    common = jnp.clip(jax.random.normal(jax.random.fold_in(key, 13), (F,), jnp.float32), -4.0, 4.0)
    values = fresh_part + amount * sign_table * common[None, None, :]
    return values.astype(jnp.bfloat16)


def shard_levels(own_key, shape, split, least, high):
    gain, own = 1.0, jax.random.fold_in(own_key, 6)
    for axis_at, parts in split:
        heights = jnp.exp(jax.random.uniform(jax.random.fold_in(own, axis_at), (parts,), jnp.float32, least / len(split), high / len(split)))
        gain = gain * jnp.repeat(heights, shape[axis_at] // parts).reshape([-1 if axis == axis_at else 1 for axis in range(len(shape))])
    return gain


def bell_draw(key, shape, deviation, bound, split=(), dtype=jnp.bfloat16):
    drawn = jax.random.normal(key, shape, jnp.float32) * deviation
    if len(split) > 0:
        drawn = shard_levels(key, shape, split, -0.22, 0.18) * drawn
    return jnp.clip(drawn, min=-bound, max=bound).astype(dtype)


def setup_inputs(seed: int = 0) -> dict:
    streams_of = jax.random.split(jax.random.key(seed), 6)
    return {
        "acts": bell_draw(streams_of[0], (POPULATION_SIZE, TOK, D), 1.0, 6.0, ((0, 4), (2, 8))),
        "weight": bell_draw(streams_of[1], (D, F), D ** -0.5, 0.09375, ((0, 4), (1, 8))),
        "input_noise_factor": draw_input_noise_factor(jax.random.fold_in(streams_of[5], 71), 0),
        "output_noise_factor": draw_output_noise_factor(jax.random.fold_in(streams_of[5], 71), 0),
        "ranks": jax.random.permutation(streams_of[4], POPULATION_SIZE).astype(jnp.int32),
    }


def reference(acts, weight, input_noise_factor, output_noise_factor, ranks):

    def member_index(items):
        tokens, left, right = items
        base = jnp.dot(tokens, weight, preferred_element_type=jnp.float32)
        lower_bound = jnp.dot(tokens, left.T, preferred_element_type=jnp.float32)
        pert = jnp.dot(lower_bound, right.astype(jnp.float32), precision=lax.Precision.HIGHEST)
        return (base + 0.5 * pert).astype(jnp.bfloat16)
    member_out = lax.map(member_index, (acts, input_noise_factor, output_noise_factor))
    fit = ranks.astype(jnp.float32) / (POPULATION_SIZE - 1) - 0.5
    scaled_update = (output_noise_factor.astype(jnp.float32) * fit[:, None, None]).astype(jnp.bfloat16)
    weight_change = jnp.einsum('vjs,vjg->sg', input_noise_factor.astype(jnp.float32), scaled_update.astype(jnp.float32), precision=lax.Precision.HIGHEST)
    mean_sq = jnp.sum(weight_change * weight_change) / (D * F)
    step_dir = weight_change * lax.rsqrt(mean_sq + 1e-06)
    new_weight = (weight.astype(jnp.float32) + 0.01 * step_dir).astype(jnp.bfloat16)
    return (member_out, step_dir, new_weight)
```

```python
import functools

import jax
import jax.numpy as jnp
from jax import lax
from jax.experimental import pallas as pl
from jax.experimental.pallas import tpu as pltpu
from jax.sharding import PartitionSpec as P

VMEM = 48 * 1024 * 1024
LANES = 128
NT = (((1,), (1,)), ((), ()))
TN = (((0,), (0,)), ((), ()))


def up(n, m):
    return -(-n // m) * m


def call(kernel, **kw):
    return pl.pallas_call(
        kernel,
        compiler_params=pltpu.CompilerParams(vmem_limit_bytes=VMEM),
        cost_estimate=pl.CostEstimate(flops=1, bytes_accessed=1, transcendentals=0),
        **kw,
    )


def low_kernel(core_ref, mine_ref, theirs_ref, inf_ref, out_ref, acc_ref, *, tok, rank):
    k = pl.program_id(0)

    @pl.when(k == 0)
    def _():
        acc_ref[...] = jnp.zeros_like(acc_ref)

    for s, acts in enumerate((mine_ref, theirs_ref)):
        acc_ref[s] += lax.dot_general(acts[...], inf_ref[...], NT, preferred_element_type=jnp.float32)

    @pl.when(k == pl.num_programs(0) - 1)
    def _():
        for s in range(2):
            full = acc_ref[s]
            rows, n = full.shape
            base = (core_ref[0] ^ s) * rows
            row = (base + lax.broadcasted_iota(jnp.int32, full.shape, 0)) // tok
            col = lax.broadcasted_iota(jnp.int32, full.shape, 1) // rank
            rest = jnp.where(row == col, 0.5 * full, 0.0)
            for i in range(3):
                part = rest.astype(jnp.bfloat16)
                out_ref[s, :, i * n : (i + 1) * n] = part
                rest = rest - part.astype(jnp.float32)


def low_terms(core, acts, inf, tok, rank):
    blocks, rows, kb = acts[0].shape
    n = inf.shape[1]
    act = pl.BlockSpec((None, rows, kb), lambda k, _: (k, 0, 0))
    return call(
        functools.partial(low_kernel, tok=tok, rank=rank),
        grid_spec=pltpu.PrefetchScalarGridSpec(
            num_scalar_prefetch=1,
            grid=(blocks,),
            in_specs=[act, act, pl.BlockSpec((None, n, kb), lambda k, _: (k, 0, 0))],
            out_specs=pl.BlockSpec((2, rows, 3 * n), lambda k, _: (0, 0, 0)),
            scratch_shapes=[pltpu.VMEM((2, rows, n), jnp.float32)],
        ),
        out_shape=jax.ShapeDtypeStruct((2, rows, 3 * n), jnp.bfloat16),
    )(core, *acts, inf)


def own_kernel(idx_ref, mine_ref, theirs_ref, weight_ref, low_ref, onf_ref, out_ref):
    del idx_ref
    for s, acts in enumerate((mine_ref, theirs_ref)):
        total = jnp.dot(low_ref[s], onf_ref[...], preferred_element_type=jnp.float32)
        out_ref[s] = total + lax.dot_general(
            acts[...], weight_ref[...], NT, preferred_element_type=jnp.float32
        )


def own_sum(block, acts, weight, low, onf, bn=512):
    _, rows, kb = acts[0].shape
    cols = weight.shape[0]
    act = pl.BlockSpec((None, rows, kb), lambda n, ref: (ref[0], 0, 0))
    return call(
        own_kernel,
        grid_spec=pltpu.PrefetchScalarGridSpec(
            num_scalar_prefetch=1,
            grid=(pl.cdiv(cols, bn),),
            in_specs=[
                act,
                act,
                pl.BlockSpec((bn, kb), lambda n, _: (n, 0)),
                pl.BlockSpec(low.shape, lambda n, _: (0, 0, 0)),
                pl.BlockSpec((onf.shape[0], bn), lambda n, _: (0, n)),
            ],
            out_specs=pl.BlockSpec((2, rows, bn), lambda n, _: (0, 0, n)),
        ),
        out_shape=jax.ShapeDtypeStruct((2, rows, cols), jnp.float32),
    )(block.reshape(1), *acts, weight, low, onf)


def near_kernel(idx_ref, acc_ref, *refs, cut, whole, split):
    del idx_ref
    count = cut + whole
    acts, wholes = refs[: 2 * count], refs[2 * count : 2 * count + whole]
    firsts = refs[2 * count + whole : 3 * count]
    seconds, out_ref = refs[3 * count : 3 * count + cut], refs[-1]

    def run(weights):
        for s in range(2):
            total = acc_ref[s]
            for i, w in enumerate(weights):
                total += lax.dot_general(
                    acts[2 * i + s][...], w[...], NT, preferred_element_type=jnp.float32
                )
            out_ref[s] = total

    pl.when(pl.program_id(0) < split)(lambda: run([*firsts, *wholes]))
    pl.when(pl.program_id(0) >= split)(lambda: run([*seconds, *wholes]))


def near_sum(blocks, acts, acc, pairs, wholes, bn):
    _, rows, kb = acts[0].shape
    cols = acc.shape[2]
    count = len(pairs) + len(wholes)
    split = pairs[0][0].shape[0] // bn
    hold = pl.BlockSpec((2, rows, bn), lambda n, _: (0, 0, n))
    specs = [hold]
    args = []
    for i in range(count):
        act = pl.BlockSpec(
            (None, rows, kb), functools.partial(lambda n, ref, i: (ref[i], 0, 0), i=i)
        )
        specs += [act, act]
        args += list(acts)
    specs += [pl.BlockSpec((bn, kb), lambda n, _: (n, 0))] * len(wholes)
    specs += [pl.BlockSpec((bn, kb), lambda n, _: (jnp.minimum(n, split - 1), 0))] * len(pairs)
    specs += [pl.BlockSpec((bn, kb), lambda n, _: (jnp.maximum(n - split, 0), 0))] * len(pairs)
    return call(
        functools.partial(near_kernel, cut=len(pairs), whole=len(wholes), split=split),
        grid_spec=pltpu.PrefetchScalarGridSpec(
            num_scalar_prefetch=1,
            grid=(pl.cdiv(cols, bn),),
            in_specs=specs,
            out_specs=hold,
        ),
        out_shape=jax.ShapeDtypeStruct((2, rows, cols), jnp.float32),
    )(jnp.stack(blocks), acc, *args, *wholes, *[p[0] for p in pairs], *[p[1] for p in pairs])


def far_kernel(idx_ref, acc_ref, *refs, count, split):
    acts, firsts = refs[: 2 * count], refs[2 * count : 3 * count]
    seconds, out_ref = refs[3 * count : 4 * count], refs[-1]
    rows = acc_ref.shape[1]

    def run(weights):
        for s in range(2):
            total = acc_ref[s]
            for i, w in enumerate(weights):
                total += lax.dot_general(
                    acts[2 * i + s][...], w[...], NT, preferred_element_type=jnp.float32
                )
            at = pl.multiple_of((idx_ref[0] ^ s) * rows, rows)
            out_ref[pl.ds(at, rows), :] = total.astype(out_ref.dtype)

    pl.when(pl.program_id(0) < split)(lambda: run(firsts))
    pl.when(pl.program_id(0) >= split)(lambda: run(seconds))


def far_sum(core, blocks, acts, acc, firsts, seconds, out, starts, bn):
    _, rows, kb = acts[0].shape
    cols = acc.shape[2]
    count = len(firsts)
    split = pl.cdiv(firsts[0].shape[0], bn)
    steps = split + pl.cdiv(seconds[0].shape[0], bn)
    base, other = starts[0] // bn, starts[1] // bn - split

    def at(n):
        return jnp.where(n < split, base + n, other + n)

    specs = [pl.BlockSpec((2, rows, bn), lambda n, _: (0, 0, at(n)))]
    args = []
    for i in range(count):
        act = pl.BlockSpec(
            (None, rows, kb), functools.partial(lambda n, ref, i: (ref[i], 0, 0), i=i + 1)
        )
        specs += [act, act]
        args += list(acts)
    specs += [pl.BlockSpec((bn, kb), lambda n, _: (jnp.minimum(n, split - 1), 0))] * count
    specs += [pl.BlockSpec((bn, kb), lambda n, _: (jnp.maximum(n - split, 0), 0))] * count
    args += firsts + seconds
    alias = {}
    if out is not None:
        specs.append(pl.BlockSpec(memory_space=pl.ANY))
        args.append(out)
        alias = {len(args) + 1: 0}
    return call(
        functools.partial(far_kernel, count=count, split=split),
        grid_spec=pltpu.PrefetchScalarGridSpec(
            num_scalar_prefetch=1,
            grid=(steps,),
            in_specs=specs,
            out_specs=pl.BlockSpec((2 * rows, bn), lambda n, _: (0, at(n))),
        ),
        out_shape=jax.ShapeDtypeStruct((2 * rows, cols), jnp.bfloat16),
        input_output_aliases=alias,
    )(jnp.concatenate([core, jnp.stack(blocks)]), acc, *args)


def square_kernel(left_ref, right_ref, out_ref, *, cols):
    n = pl.program_id(0)
    delta = lax.dot_general(
        right_ref[...], left_ref[...], TN, preferred_element_type=jnp.float32
    )
    at = n * delta.shape[0] + lax.broadcasted_iota(jnp.int32, delta.shape, 0)
    delta = jnp.where(at < cols, delta, 0.0)

    @pl.when(n == 0)
    def _():
        out_ref[...] = jnp.zeros_like(out_ref)

    part = jnp.sum((delta * delta).reshape(-1, 8, delta.shape[1]), axis=0)
    for j in range(0, delta.shape[1], LANES):
        out_ref[...] += part[:, j : j + LANES]


def sum_squares(factors, wide, cols):
    k = factors.shape[0]
    return call(
        functools.partial(square_kernel, cols=cols),
        grid=(pl.cdiv(cols, wide),),
        in_specs=[
            pl.BlockSpec((k, wide), lambda n: (0, 0)),
            pl.BlockSpec((k, wide), lambda n: (0, n + 1)),
        ],
        out_specs=pl.BlockSpec((8, LANES), lambda n: (0, 0)),
        out_shape=jax.ShapeDtypeStruct((8, LANES), jnp.float32),
    )(factors, factors)


def step_kernel(sums_ref, left_ref, right_ref, weight_ref, step_ref, new_ref, *, count):
    mean_sq = jnp.sum(sums_ref[...]) / count
    scale = lax.rsqrt(jnp.full((1, 1), mean_sq + 1e-06, jnp.float32))
    delta = lax.dot_general(
        right_ref[...], left_ref[...], TN, preferred_element_type=jnp.float32
    )
    step = delta[:, : step_ref.shape[1]] * scale
    step_ref[...] = step
    new_ref[...] = (weight_ref[...].astype(jnp.float32) + 0.01 * step).astype(new_ref.dtype)


def apply_step(sums, factors, wide, weight, count):
    cols, rows = weight.shape
    k = factors.shape[0]
    block = pl.BlockSpec((wide, rows), lambda n: (n, 0))
    return call(
        functools.partial(step_kernel, count=count),
        grid=(pl.cdiv(cols, wide),),
        in_specs=[
            pl.BlockSpec(sums.shape, lambda n: (0, 0)),
            pl.BlockSpec((k, wide), lambda n: (0, 0)),
            pl.BlockSpec((k, wide), lambda n: (0, n + 1)),
            block,
        ],
        out_specs=[block, block],
        out_shape=[
            jax.ShapeDtypeStruct((cols, rows), jnp.float32),
            jax.ShapeDtypeStruct((cols, rows), weight.dtype),
        ],
    )(sums, factors, factors, weight)


def body(acts, weight, input_noise_factor, output_noise_factor, ranks):
    members, tok, kb = acts.shape
    rank, width = input_noise_factor.shape[1:]
    pops, cols = lax.axis_size("pop"), lax.axis_size("col")
    ny, cores = 2, 2
    nx = pops // ny
    total_members = members * pops
    local = output_noise_factor.shape[2]
    rows = width // pops
    factors_here = members * rank
    pop = lax.axis_index("pop").astype(jnp.int32)
    core = lax.rem(lax.axis_index("col").astype(jnp.int32), cores)
    y, x = pop // nx, lax.rem(pop, nx)

    def place(dy, dx):
        return lax.rem(y + dy, ny) * nx + lax.rem(x + nx - dx, nx)

    def move(v, dy, dx):
        route = [(i, (i // nx + dy) % ny * nx + (i + dx) % nx) for i in range(pops)]
        return lax.ppermute(v, "pop", route)

    other_core = [(i, i ^ 1) for i in range(cols)]

    wide = up(rows, LANES)
    fit = ranks.astype(jnp.float32) / (total_members - 1) - 0.5
    scaled = (output_noise_factor.astype(jnp.float32) * fit[:, None, None]).astype(jnp.bfloat16)
    scaled = scaled.reshape(factors_here, local)
    inf = input_noise_factor.reshape(factors_here, width)

    def rows_for(dy, dx):
        target = lax.rem(y + dy, ny) * nx + lax.rem(x + dx, nx)
        part = lax.dynamic_slice_in_dim(inf, target * rows, rows, axis=1)
        return jnp.pad(part, ((0, 0), (0, wide - rows)))

    join = lambda *parts: jnp.concatenate(parts, axis=1)
    held = {(0, 0): join(rows_for(0, 0), scaled)}
    along_y = move(join(*[rows_for(1, dx) for dx in range(nx)], scaled), 1, 0)
    for dx in range(1, nx):
        held[0, dx] = move(join(rows_for(0, dx), scaled), 0, dx)
    along_y, near_x = lax.optimization_barrier((along_y, [held[0, dx] for dx in range(1, nx)]))
    for dx in range(1, nx):
        held[0, dx] = near_x[dx - 1]
    tail = along_y[:, nx * wide :]
    held[1, 0] = join(along_y[:, :wide], tail)
    for dx in range(1, nx):
        held[1, dx] = move(join(along_y[:, dx * wide : (dx + 1) * wide], tail), 0, dx)

    flat = acts.reshape(members * tok, kb)
    half = members * tok // cores
    mine = lax.dynamic_slice_in_dim(flat, core * half, half, axis=0)
    theirs = lax.dynamic_slice_in_dim(flat, (1 - core) * half, half, axis=0)
    theirs = lax.ppermute(theirs, "col", other_core)
    slab = jnp.where(core == 0, join(mine, theirs), join(theirs, mine))
    groups = [[i for i in range(cols) if i % cores == c] for c in range(cores)]
    acts_mine = lax.all_gather(slab, "col", axis=0, axis_index_groups=groups)
    if acts_mine.shape[0] != pops:
        acts_mine = acts_mine.reshape(pops, -1, half, acts_mine.shape[2])
        acts_mine = acts_mine.transpose(0, 2, 1, 3).reshape(pops, half, rows)

    order = [(dy, dx) for dy in range(ny) for dx in range(nx)]
    factors = jnp.concatenate([held[o] for o in order], axis=0)
    sums = sum_squares(factors, wide, local)
    reach = 1
    while reach < cols:
        sums = sums + lax.ppermute(sums, "col", [(i, i ^ reach) for i in range(cols)])
        reach *= 2

    bn = 256
    wt = weight.T
    cut = -(-local // (2 * bn)) * bn
    to_y, _ = lax.optimization_barrier((wt, along_y))
    to_x, _ = lax.optimization_barrier(((wt[:cut], wt[cut:]), held[1, 1]))
    from_y = move(to_y, 1, 0)
    from_x = {0: to_x}
    for dx in range(1, nx):
        from_x[dx] = [move(v, 0, 1) for v in from_x[dx - 1]]

    core_at = core.reshape(1)
    (acts_mine, sums), from_x[1][0] = lax.optimization_barrier(((acts_mine, sums), from_x[1][0]))
    acts_all = (acts_mine, lax.ppermute(acts_mine, "col", other_core))
    inf_blocks = inf.reshape(factors_here, pops, rows).transpose(1, 0, 2)
    low = low_terms(core_at, acts_all, inf_blocks, tok, rank)
    onf = output_noise_factor.reshape(factors_here, local)
    onf = jnp.concatenate([onf] * 3, axis=0)
    acc = own_sum(place(0, 0), acts_all, wt, low, onf)

    def parts(lo, hi):
        mid = lo + (pl.cdiv(hi - lo, bn) + 1) // 2 * bn
        return [(lo, mid), (mid, hi)]

    cuts = list(zip(parts(0, cut), parts(cut, local)))
    sums = sums + move(sums, 1, 0)
    to_y = [[from_x[dx][0][lo:hi] for dx in range(1, nx)] for (lo, hi), _ in cuts]
    to_y, acc, sums = lax.optimization_barrier((to_y, acc, sums))
    last_y = [[move(v, 1, 0) for v in part] for part in to_y]
    sums = sum([move(sums, 0, dx) for dx in range(1, nx)], sums)
    to_x = [from_y[lo:hi] for _, (lo, hi) in cuts]
    to_x, sums = lax.optimization_barrier((to_x, sums))
    last_x = []
    for run in to_x:
        last_x.append([])
        for dx in range(1, nx):
            run = move(run, 0, 1)
            last_x[-1].append(run)

    near = [(0, dx) for dx in range(1, nx)]
    acc = near_sum(
        [place(*o) for o in near + [(1, 0)]], acts_all, acc, [from_x[dx] for _, dx in near], [from_y], bn
    )
    acc, sums = lax.optimization_barrier((acc, sums))
    step_dir, new_weight = apply_step(sums, factors, wide, wt, width * local * cols)
    out = None
    blocks = [place(1, dx) for dx in range(1, nx)]
    for ((a, _), (b, _)), firsts, seconds in zip(cuts, last_y, last_x):
        out = far_sum(core_at, blocks, acts_all, acc, firsts, seconds, out, (a, b), bn)
    return out.reshape(members, tok, local), step_dir.T, new_weight.T


def solution(mesh):
    in_specs = (
        P("pop", None, "col"),
        P("pop", "col"),
        P("pop", None, None),
        P("pop", None, "col"),
        P("pop"),
    )
    out_specs = (P("pop", None, "col"), P("pop", "col"), P("pop", "col"))
    return jax.shard_map(body, mesh=mesh, in_specs=in_specs, out_specs=out_specs, check_vma=False)
```

```python
import functools

import jax
import jax.numpy as jnp
from jax import lax
from jax.experimental import pallas as pl
from jax.experimental.pallas import tpu as pltpu
from jax.sharding import PartitionSpec as P

VMEM = 36 * 1024 * 1024
LANES = 128
NT = (((1,), (1,)), ((), ()))
TN = (((0,), (0,)), ((), ()))


def up(n, m):
    return -(-n // m) * m


def call(kernel, vmem=VMEM, **kw):
    return pl.pallas_call(
        kernel,
        compiler_params=pltpu.CompilerParams(vmem_limit_bytes=vmem),
        cost_estimate=pl.CostEstimate(flops=1, bytes_accessed=1, transcendentals=0),
        **kw,
    )


def low_kernel(core_ref, mine_ref, theirs_ref, inf_ref, out_ref, acc_ref, *, tok, rank):
    k = pl.program_id(0)

    @pl.when(k == 0)
    def _():
        acc_ref[...] = jnp.zeros_like(acc_ref)

    for s, acts in enumerate((mine_ref, theirs_ref)):
        acc_ref[s] += lax.dot_general(acts[...], inf_ref[...], NT, preferred_element_type=jnp.float32)

    @pl.when(k == pl.num_programs(0) - 1)
    def _():
        for s in range(2):
            full = acc_ref[s]
            rows, n = full.shape
            base = (core_ref[0] ^ s) * rows
            row = (base + lax.broadcasted_iota(jnp.int32, full.shape, 0)) // tok
            col = lax.broadcasted_iota(jnp.int32, full.shape, 1) // rank
            rest = jnp.where(row == col, 0.5 * full, 0.0)
            for i in range(3):
                part = rest.astype(jnp.bfloat16)
                out_ref[s, :, i * n : (i + 1) * n] = part
                rest = rest - part.astype(jnp.float32)


def low_terms(core, acts, inf, tok, rank):
    blocks, rows, kb = acts[0].shape
    n = inf.shape[1]
    act = pl.BlockSpec((None, rows, kb), lambda k, _: (k, 0, 0))
    return call(
        functools.partial(low_kernel, tok=tok, rank=rank),
        grid_spec=pltpu.PrefetchScalarGridSpec(
            num_scalar_prefetch=1,
            grid=(blocks,),
            in_specs=[act, act, pl.BlockSpec((None, n, kb), lambda k, _: (k, 0, 0))],
            out_specs=pl.BlockSpec((2, rows, 3 * n), lambda k, _: (0, 0, 0)),
            scratch_shapes=[pltpu.VMEM((2, rows, n), jnp.float32)],
        ),
        out_shape=jax.ShapeDtypeStruct((2, rows, 3 * n), jnp.bfloat16),
    )(core, *acts, inf)


def near_kernel(idx_ref, low_ref, onf_ref, *refs, count):
    del idx_ref
    acts, weights, out_ref = refs[: 2 * count], refs[2 * count : 3 * count], refs[-1]
    for s in range(2):
        total = jnp.dot(low_ref[s], onf_ref[...], preferred_element_type=jnp.float32)
        for i, w in enumerate(weights):
            total += lax.dot_general(
                acts[2 * i + s][...], w[...], NT, preferred_element_type=jnp.float32
            )
        out_ref[s] = total


def near_sum(blocks, acts, low, onf, weights, bn=512):
    _, rows, kb = acts[0].shape
    cols = weights[0].shape[0]
    count = len(weights)
    specs = [
        pl.BlockSpec(low.shape, lambda n, _: (0, 0, 0)),
        pl.BlockSpec((onf.shape[0], bn), lambda n, _: (0, n)),
    ]
    args = []
    for i in range(count):
        act = pl.BlockSpec(
            (None, rows, kb), functools.partial(lambda n, ref, i: (ref[i], 0, 0), i=i)
        )
        specs += [act, act]
        args += list(acts)
    specs += [pl.BlockSpec((bn, kb), lambda n, _: (n, 0))] * count
    return call(
        functools.partial(near_kernel, count=count),
        vmem=40 * 1024 * 1024,
        grid_spec=pltpu.PrefetchScalarGridSpec(
            num_scalar_prefetch=1,
            grid=(pl.cdiv(cols, bn),),
            in_specs=specs,
            out_specs=pl.BlockSpec((2, rows, bn), lambda n, _: (0, 0, n)),
        ),
        out_shape=jax.ShapeDtypeStruct((2, rows, cols), jnp.float32),
    )(jnp.stack(blocks), low, onf, *args, *weights)


def far_kernel(at_ref, idx_ref, acc_ref, *refs, count, split):
    del at_ref
    acts, firsts = refs[: 2 * count], refs[2 * count : 3 * count]
    seconds, out_ref = refs[3 * count : 4 * count], refs[-1]
    rows = acc_ref.shape[1]

    def run(weights):
        for s in range(2):
            total = acc_ref[s]
            for i, w in enumerate(weights):
                total += lax.dot_general(
                    acts[2 * i + s][...], w[...], NT, preferred_element_type=jnp.float32
                )
            at = pl.multiple_of((idx_ref[0] ^ s) * rows, rows)
            out_ref[pl.ds(at, rows), :] = total.astype(out_ref.dtype)

    pl.when(pl.program_id(0) < split)(lambda: run(firsts))
    pl.when(pl.program_id(0) >= split)(lambda: run(seconds))


def far_sum(core, at, blocks, acts, acc, firsts, seconds, out, bn):
    _, rows, kb = acts[0].shape
    cols = acc.shape[2]
    count = len(firsts)
    split = firsts[0].shape[0] // bn
    specs = [pl.BlockSpec((2, rows, bn), lambda n, at, _: (0, 0, at[n]))]
    args = []
    for i in range(count):
        act = pl.BlockSpec(
            (None, rows, kb), functools.partial(lambda n, at, ref, i: (ref[i], 0, 0), i=i + 1)
        )
        specs += [act, act]
        args += list(acts)
    specs += [pl.BlockSpec((bn, kb), lambda n, at, _: (jnp.minimum(n, split - 1), 0))] * count
    specs += [pl.BlockSpec((bn, kb), lambda n, at, _: (jnp.maximum(n - split, 0), 0))] * count
    args += firsts + seconds
    alias = {}
    if out is not None:
        specs.append(pl.BlockSpec(memory_space=pl.ANY))
        args.append(out)
        alias = {len(args) + 2: 0}
    return call(
        functools.partial(far_kernel, count=count, split=split),
        vmem=56 * 1024 * 1024,
        grid_spec=pltpu.PrefetchScalarGridSpec(
            num_scalar_prefetch=2,
            grid=(len(at),),
            in_specs=specs,
            out_specs=pl.BlockSpec((2 * rows, bn), lambda n, at, _: (0, at[n])),
        ),
        out_shape=jax.ShapeDtypeStruct((2 * rows, cols), jnp.bfloat16),
        input_output_aliases=alias,
    )(jnp.array(at, jnp.int32), jnp.concatenate([core, jnp.stack(blocks)]), acc, *args)


def square_kernel(left_ref, right_ref, out_ref, *, cols):
    n = pl.program_id(0)
    delta = lax.dot_general(
        right_ref[...], left_ref[...], TN, preferred_element_type=jnp.float32
    )
    at = n * delta.shape[0] + lax.broadcasted_iota(jnp.int32, delta.shape, 0)
    delta = jnp.where(at < cols, delta, 0.0)

    @pl.when(n == 0)
    def _():
        out_ref[...] = jnp.zeros_like(out_ref)

    part = jnp.sum((delta * delta).reshape(-1, 8, delta.shape[1]), axis=0)
    for j in range(0, delta.shape[1], LANES):
        out_ref[...] += part[:, j : j + LANES]


def sum_squares(factors, wide, cols):
    k = factors.shape[0]
    return call(
        functools.partial(square_kernel, cols=cols),
        grid=(pl.cdiv(cols, wide),),
        in_specs=[
            pl.BlockSpec((k, wide), lambda n: (0, 0)),
            pl.BlockSpec((k, wide), lambda n: (0, n + 1)),
        ],
        out_specs=pl.BlockSpec((8, LANES), lambda n: (0, 0)),
        out_shape=jax.ShapeDtypeStruct((8, LANES), jnp.float32),
    )(factors, factors)


def step_kernel(sums_ref, left_ref, right_ref, weight_ref, step_ref, new_ref, *, count):
    mean_sq = jnp.sum(sums_ref[...]) / count
    scale = lax.rsqrt(jnp.full((1, 1), mean_sq + 1e-06, jnp.float32))
    delta = lax.dot_general(
        right_ref[...], left_ref[...], TN, preferred_element_type=jnp.float32
    )
    step = delta[:, : step_ref.shape[1]] * scale
    step_ref[...] = step
    new_ref[...] = (weight_ref[...].astype(jnp.float32) + 0.01 * step).astype(new_ref.dtype)


def apply_step(sums, factors, wide, weight, count):
    cols, rows = weight.shape
    k = factors.shape[0]
    block = pl.BlockSpec((wide, rows), lambda n: (n, 0))
    return call(
        functools.partial(step_kernel, count=count),
        grid=(pl.cdiv(cols, wide),),
        in_specs=[
            pl.BlockSpec(sums.shape, lambda n: (0, 0)),
            pl.BlockSpec((k, wide), lambda n: (0, 0)),
            pl.BlockSpec((k, wide), lambda n: (0, n + 1)),
            block,
        ],
        out_specs=[block, block],
        out_shape=[
            jax.ShapeDtypeStruct((cols, rows), jnp.float32),
            jax.ShapeDtypeStruct((cols, rows), weight.dtype),
        ],
    )(sums, factors, factors, weight)


def body(acts, weight, input_noise_factor, output_noise_factor, ranks):
    members, tok, kb = acts.shape
    rank, width = input_noise_factor.shape[1:]
    pops, cols = lax.axis_size("pop"), lax.axis_size("col")
    ny, cores = 2, 2
    nx = pops // ny
    total_members = members * pops
    local = output_noise_factor.shape[2]
    rows = width // pops
    factors_here = members * rank
    pop = lax.axis_index("pop").astype(jnp.int32)
    core = lax.rem(lax.axis_index("col").astype(jnp.int32), cores)
    y, x = pop // nx, lax.rem(pop, nx)

    def place(dy, dx):
        source = lax.rem(y + dy, ny) * nx + lax.rem(x + nx - dx, nx)
        return lax.rem(lax.axis_index("col").astype(jnp.int32) // cores + pops - source, pops)

    def move(v, dy, dx):
        route = [(i, (i // nx + dy) % ny * nx + (i + dx) % nx) for i in range(pops)]
        return lax.ppermute(v, "pop", route)

    other_core = [(i, i ^ 1) for i in range(cols)]

    wide = up(rows, LANES)
    fit = ranks.astype(jnp.float32) / (total_members - 1) - 0.5
    scaled = (output_noise_factor.astype(jnp.float32) * fit[:, None, None]).astype(jnp.bfloat16)
    scaled = scaled.reshape(factors_here, local)
    inf = input_noise_factor.reshape(factors_here, width)

    def rows_for(dy, dx):
        target = lax.rem(y + dy, ny) * nx + lax.rem(x + dx, nx)
        part = lax.dynamic_slice_in_dim(inf, target * rows, rows, axis=1)
        return jnp.pad(part, ((0, 0), (0, wide - rows)))

    join = lambda *parts: jnp.concatenate(parts, axis=1)
    order = [(dy, dx) for dy in range(ny) for dx in range(nx)]
    payloads = [join(rows_for(*o), scaled) for o in order]
    arrived = [move(v, *o) for v, o in zip(payloads[1:], order[1:])]

    flat = acts.reshape(members * tok, kb)
    half = members * tok // cores
    mine = lax.dynamic_slice_in_dim(flat, core * half, half, axis=0)
    theirs = lax.dynamic_slice_in_dim(flat, (1 - core) * half, half, axis=0)
    theirs = lax.ppermute(theirs, "col", other_core)
    slab = jnp.where(core == 0, join(mine, theirs), join(theirs, mine))
    depth = cols // cores
    assert depth == pops
    here = lax.axis_index("col").astype(jnp.int32) // cores
    inf_blocks = inf.reshape(factors_here, pops, rows).transpose(1, 0, 2)
    inf_blocks = inf_blocks[lax.rem(here + pops - jnp.arange(pops, dtype=jnp.int32), pops)]
    turn = lambda k: [(i, (i + k * cores) % cols) for i in range(cols)]
    turned = [lax.ppermute(slab, "col", turn(k)) for k in range(1, depth)]
    arrived, inf_blocks = lax.optimization_barrier((arrived, inf_blocks))

    wt = weight.T
    cut = round(local / 2 / LANES) * LANES
    last = cut + up(local - cut, LANES)
    edges_y = [0, cut - 3 * LANES, cut]
    edges_x = [cut, last - 4 * LANES, local]
    ends = list(zip(zip(edges_y, edges_y[1:]), zip(edges_x, edges_x[1:])))
    sent, arrived = lax.optimization_barrier((wt, arrived))
    from_y, from_x = move(sent, 1, 0), {0: sent}
    for dx in range(1, nx):
        from_x[dx] = move(from_x[dx - 1], 0, 1)

    arrived, turned = lax.optimization_barrier((arrived, turned))
    acts_mine = jnp.stack([slab, *turned])
    factors = jnp.concatenate([payloads[0], *arrived], axis=0)
    sums = sum_squares(factors, wide, local)
    reach = 1
    while reach < cols:
        sums = sums + lax.ppermute(sums, "col", [(i, i ^ reach) for i in range(cols)])
        reach *= 2

    core_at = core.reshape(1)
    acts_all = (acts_mine, lax.ppermute(acts_mine, "col", other_core))
    low = low_terms(core_at, acts_all, inf_blocks, tok, rank)
    onf = output_noise_factor.reshape(factors_here, local)
    onf = jnp.concatenate([onf] * 3, axis=0)
    low, sums = lax.optimization_barrier((low, sums))
    everywhere = [move(sums, *o) for o in order[1:]]
    from_x, from_y, everywhere = lax.optimization_barrier((from_x, from_y, everywhere))
    sums = sum(everywhere, sums)
    along_x = [from_x[dx] for dx in range(1, nx)]
    to_y = [[v[lo:hi] for v in along_x] for (lo, hi), _ in ends]
    to_x = [from_y[lo:hi] for _, (lo, hi) in ends]
    last_y, last_x = [], []
    for firsts, run in zip(to_y, to_x):
        last_y.append([move(v, 1, 0) for v in firsts])
        last_x.append([])
        for dx in range(1, nx):
            run = move(run, 0, 1)
            last_x[-1].append(run)
    step_dir, new_weight = apply_step(sums, factors, wide, wt, width * local * cols)

    near = [place(0, dx) for dx in range(nx)] + [place(1, 0)]
    acc = near_sum(near, acts_all, low, onf, [wt, *along_x, from_y])
    out = None
    blocks = [place(1, dx) for dx in range(1, nx)]
    for ((lo, hi), (also_lo, also_hi)), firsts, seconds in zip(ends, last_y, last_x):
        bn = next(n for n in (384, LANES) if lo % n == hi % n == also_lo % n == 0)
        at = [*range(lo // bn, hi // bn), *range(also_lo // bn, pl.cdiv(also_hi, bn))]
        out = far_sum(core_at, at, blocks, acts_all, acc, firsts, seconds, out, bn)
    return out.reshape(members, tok, local), step_dir.T, new_weight.T


def solution(mesh):
    in_specs = (
        P("pop", None, "col"),
        P("pop", "col"),
        P("pop", None, None),
        P("pop", None, "col"),
        P("pop"),
    )
    out_specs = (P("pop", None, "col"), P("pop", "col"), P("pop", "col"))
    return jax.shard_map(body, mesh=mesh, in_specs=in_specs, out_specs=out_specs, check_vma=False)
```

```python
import functools

import jax
import jax.numpy as jnp
from jax import lax
from jax.experimental import pallas as pl
from jax.experimental.pallas import tpu as pltpu
from jax.sharding import PartitionSpec as P

VMEM = 36 * 1024 * 1024
LANES = 128
NT = (((1,), (1,)), ((), ()))
TN = (((0,), (0,)), ((), ()))


def up(n, m):
    return -(-n // m) * m


def call(kernel, vmem=VMEM, **kw):
    return pl.pallas_call(
        kernel,
        compiler_params=pltpu.CompilerParams(vmem_limit_bytes=vmem),
        cost_estimate=pl.CostEstimate(flops=1, bytes_accessed=1, transcendentals=0),
        **kw,
    )


def low_kernel(core_ref, mine_ref, theirs_ref, inf_ref, out_ref, acc_ref, *, tok, rank):
    k = pl.program_id(0)

    @pl.when(k == 0)
    def _():
        acc_ref[...] = jnp.zeros_like(acc_ref)

    for s, acts in enumerate((mine_ref, theirs_ref)):
        acc_ref[s] += lax.dot_general(acts[...], inf_ref[...], NT, preferred_element_type=jnp.float32)

    @pl.when(k == pl.num_programs(0) - 1)
    def _():
        for s in range(2):
            full = acc_ref[s]
            rows, n = full.shape
            base = (core_ref[0] ^ s) * rows
            row = (base + lax.broadcasted_iota(jnp.int32, full.shape, 0)) // tok
            col = lax.broadcasted_iota(jnp.int32, full.shape, 1) // rank
            rest = jnp.where(row == col, 0.5 * full, 0.0)
            for i in range(3):
                part = rest.astype(jnp.bfloat16)
                out_ref[s, :, i * n : (i + 1) * n] = part
                rest = rest - part.astype(jnp.float32)


def low_terms(core, acts, inf, tok, rank):
    blocks, rows, kb = acts[0].shape
    n = inf.shape[1]
    act = pl.BlockSpec((None, rows, kb), lambda k, _: (k, 0, 0))
    return call(
        functools.partial(low_kernel, tok=tok, rank=rank),
        grid_spec=pltpu.PrefetchScalarGridSpec(
            num_scalar_prefetch=1,
            grid=(blocks,),
            in_specs=[act, act, pl.BlockSpec((None, n, kb), lambda k, _: (k, 0, 0))],
            out_specs=pl.BlockSpec((2, rows, 3 * n), lambda k, _: (0, 0, 0)),
            scratch_shapes=[pltpu.VMEM((2, rows, n), jnp.float32)],
        ),
        out_shape=jax.ShapeDtypeStruct((2, rows, 3 * n), jnp.bfloat16),
    )(core, *acts, inf)


def own_kernel(idx_ref, mine_ref, theirs_ref, weight_ref, low_ref, onf_ref, out_ref):
    del idx_ref
    for s, acts in enumerate((mine_ref, theirs_ref)):
        total = jnp.dot(low_ref[s], onf_ref[...], preferred_element_type=jnp.float32)
        out_ref[s] = total + lax.dot_general(
            acts[...], weight_ref[...], NT, preferred_element_type=jnp.float32
        )


def own_sum(block, acts, weight, low, onf, bn=512):
    _, rows, kb = acts[0].shape
    cols = weight.shape[0]
    act = pl.BlockSpec((None, rows, kb), lambda n, ref: (ref[0], 0, 0))
    return call(
        own_kernel,
        grid_spec=pltpu.PrefetchScalarGridSpec(
            num_scalar_prefetch=1,
            grid=(pl.cdiv(cols, bn),),
            in_specs=[
                act,
                act,
                pl.BlockSpec((bn, kb), lambda n, _: (n, 0)),
                pl.BlockSpec(low.shape, lambda n, _: (0, 0, 0)),
                pl.BlockSpec((onf.shape[0], bn), lambda n, _: (0, n)),
            ],
            out_specs=pl.BlockSpec((2, rows, bn), lambda n, _: (0, 0, n)),
        ),
        out_shape=jax.ShapeDtypeStruct((2, rows, cols), jnp.float32),
    )(block.reshape(1), *acts, weight, low, onf)


def near_kernel(idx_ref, acc_ref, *refs, count):
    del idx_ref
    acts, weights, out_ref = refs[: 2 * count], refs[2 * count : 3 * count], refs[-1]
    for s in range(2):
        total = acc_ref[s]
        for i, w in enumerate(weights):
            total += lax.dot_general(
                acts[2 * i + s][...], w[...], NT, preferred_element_type=jnp.float32
            )
        out_ref[s] = total


def near_sum(blocks, acts, acc, weights, bn=512):
    _, rows, kb = acts[0].shape
    cols = weights[0].shape[0]
    count = len(weights)
    specs = [pl.BlockSpec((2, rows, bn), lambda n, _: (0, 0, n))]
    args = []
    for i in range(count):
        act = pl.BlockSpec(
            (None, rows, kb), functools.partial(lambda n, ref, i: (ref[i], 0, 0), i=i)
        )
        specs += [act, act]
        args += list(acts)
    specs += [pl.BlockSpec((bn, kb), lambda n, _: (n, 0))] * count
    return call(
        functools.partial(near_kernel, count=count),
        vmem=40 * 1024 * 1024,
        grid_spec=pltpu.PrefetchScalarGridSpec(
            num_scalar_prefetch=1,
            grid=(pl.cdiv(cols, bn),),
            in_specs=specs,
            out_specs=pl.BlockSpec((2, rows, bn), lambda n, _: (0, 0, n)),
        ),
        out_shape=jax.ShapeDtypeStruct((2, rows, cols), jnp.float32),
    )(jnp.stack(blocks), acc, *args, *weights)


def far_kernel(at_ref, idx_ref, acc_ref, *refs, count, split):
    del at_ref
    acts, firsts = refs[: 2 * count], refs[2 * count : 3 * count]
    seconds, out_ref = refs[3 * count : 4 * count], refs[-1]
    rows = acc_ref.shape[1]

    def run(weights):
        for s in range(2):
            total = acc_ref[s]
            for i, w in enumerate(weights):
                total += lax.dot_general(
                    acts[2 * i + s][...], w[...], NT, preferred_element_type=jnp.float32
                )
            at = pl.multiple_of((idx_ref[0] ^ s) * rows, rows)
            out_ref[pl.ds(at, rows), :] = total.astype(out_ref.dtype)

    pl.when(pl.program_id(0) < split)(lambda: run(firsts))
    pl.when(pl.program_id(0) >= split)(lambda: run(seconds))


def far_sum(core, at, blocks, acts, acc, firsts, seconds, out, bn):
    _, rows, kb = acts[0].shape
    cols = acc.shape[2]
    count = len(firsts)
    split = firsts[0].shape[0] // bn
    specs = [pl.BlockSpec((2, rows, bn), lambda n, at, _: (0, 0, at[n]))]
    args = []
    for i in range(count):
        act = pl.BlockSpec(
            (None, rows, kb), functools.partial(lambda n, at, ref, i: (ref[i], 0, 0), i=i + 1)
        )
        specs += [act, act]
        args += list(acts)
    specs += [pl.BlockSpec((bn, kb), lambda n, at, _: (jnp.minimum(n, split - 1), 0))] * count
    specs += [pl.BlockSpec((bn, kb), lambda n, at, _: (jnp.maximum(n - split, 0), 0))] * count
    args += firsts + seconds
    alias = {}
    if out is not None:
        specs.append(pl.BlockSpec(memory_space=pl.ANY))
        args.append(out)
        alias = {len(args) + 2: 0}
    return call(
        functools.partial(far_kernel, count=count, split=split),
        vmem=56 * 1024 * 1024,
        grid_spec=pltpu.PrefetchScalarGridSpec(
            num_scalar_prefetch=2,
            grid=(len(at),),
            in_specs=specs,
            out_specs=pl.BlockSpec((2 * rows, bn), lambda n, at, _: (0, at[n])),
        ),
        out_shape=jax.ShapeDtypeStruct((2 * rows, cols), jnp.bfloat16),
        input_output_aliases=alias,
    )(jnp.array(at, jnp.int32), jnp.concatenate([core, jnp.stack(blocks)]), acc, *args)


def square_kernel(left_ref, right_ref, out_ref, *, cols):
    n = pl.program_id(0)
    delta = lax.dot_general(
        right_ref[...], left_ref[...], TN, preferred_element_type=jnp.float32
    )
    at = n * delta.shape[0] + lax.broadcasted_iota(jnp.int32, delta.shape, 0)
    delta = jnp.where(at < cols, delta, 0.0)

    @pl.when(n == 0)
    def _():
        out_ref[...] = jnp.zeros_like(out_ref)

    part = jnp.sum((delta * delta).reshape(-1, 8, delta.shape[1]), axis=0)
    for j in range(0, delta.shape[1], LANES):
        out_ref[...] += part[:, j : j + LANES]


def sum_squares(factors, wide, cols):
    k = factors.shape[0]
    return call(
        functools.partial(square_kernel, cols=cols),
        grid=(pl.cdiv(cols, wide),),
        in_specs=[
            pl.BlockSpec((k, wide), lambda n: (0, 0)),
            pl.BlockSpec((k, wide), lambda n: (0, n + 1)),
        ],
        out_specs=pl.BlockSpec((8, LANES), lambda n: (0, 0)),
        out_shape=jax.ShapeDtypeStruct((8, LANES), jnp.float32),
    )(factors, factors)


def step_kernel(sums_ref, left_ref, right_ref, weight_ref, step_ref, new_ref, *, count):
    mean_sq = jnp.sum(sums_ref[...]) / count
    scale = lax.rsqrt(jnp.full((1, 1), mean_sq + 1e-06, jnp.float32))
    delta = lax.dot_general(
        right_ref[...], left_ref[...], TN, preferred_element_type=jnp.float32
    )
    step = delta[:, : step_ref.shape[1]] * scale
    step_ref[...] = step
    new_ref[...] = (weight_ref[...].astype(jnp.float32) + 0.01 * step).astype(new_ref.dtype)


def apply_step(sums, factors, wide, weight, count):
    cols, rows = weight.shape
    k = factors.shape[0]
    block = pl.BlockSpec((wide, rows), lambda n: (n, 0))
    return call(
        functools.partial(step_kernel, count=count),
        grid=(pl.cdiv(cols, wide),),
        in_specs=[
            pl.BlockSpec(sums.shape, lambda n: (0, 0)),
            pl.BlockSpec((k, wide), lambda n: (0, 0)),
            pl.BlockSpec((k, wide), lambda n: (0, n + 1)),
            block,
        ],
        out_specs=[block, block],
        out_shape=[
            jax.ShapeDtypeStruct((cols, rows), jnp.float32),
            jax.ShapeDtypeStruct((cols, rows), weight.dtype),
        ],
    )(sums, factors, factors, weight)


def body(acts, weight, input_noise_factor, output_noise_factor, ranks):
    members, tok, kb = acts.shape
    rank, width = input_noise_factor.shape[1:]
    pops, cols = lax.axis_size("pop"), lax.axis_size("col")
    ny, cores = 2, 2
    nx = pops // ny
    total_members = members * pops
    local = output_noise_factor.shape[2]
    rows = width // pops
    factors_here = members * rank
    pop = lax.axis_index("pop").astype(jnp.int32)
    core = lax.rem(lax.axis_index("col").astype(jnp.int32), cores)
    y, x = pop // nx, lax.rem(pop, nx)

    def place(dy, dx):
        source = lax.rem(y + dy, ny) * nx + lax.rem(x + nx - dx, nx)
        return lax.rem(lax.axis_index("col").astype(jnp.int32) // cores + pops - source, pops)

    def move(v, dy, dx):
        route = [(i, (i // nx + dy) % ny * nx + (i + dx) % nx) for i in range(pops)]
        return lax.ppermute(v, "pop", route)

    other_core = [(i, i ^ 1) for i in range(cols)]

    wide = up(rows, LANES)
    fit = ranks.astype(jnp.float32) / (total_members - 1) - 0.5
    scaled = (output_noise_factor.astype(jnp.float32) * fit[:, None, None]).astype(jnp.bfloat16)
    scaled = scaled.reshape(factors_here, local)
    inf = input_noise_factor.reshape(factors_here, width)

    def rows_for(dy, dx):
        target = lax.rem(y + dy, ny) * nx + lax.rem(x + dx, nx)
        part = lax.dynamic_slice_in_dim(inf, target * rows, rows, axis=1)
        return jnp.pad(part, ((0, 0), (0, wide - rows)))

    join = lambda *parts: jnp.concatenate(parts, axis=1)
    order = [(dy, dx) for dy in range(ny) for dx in range(nx)]
    payloads = [join(rows_for(*o), scaled) for o in order]

    flat = acts.reshape(members * tok, kb)
    half = members * tok // cores
    mine = lax.dynamic_slice_in_dim(flat, core * half, half, axis=0)
    theirs = lax.dynamic_slice_in_dim(flat, (1 - core) * half, half, axis=0)
    theirs = lax.ppermute(theirs, "col", other_core)
    slab = jnp.where(core == 0, join(mine, theirs), join(theirs, mine))
    depth = cols // cores
    assert depth == pops
    here = lax.axis_index("col").astype(jnp.int32) // cores
    inf_blocks = inf.reshape(factors_here, pops, rows).transpose(1, 0, 2)
    inf_blocks = inf_blocks[lax.rem(here + pops - jnp.arange(pops, dtype=jnp.int32), pops)]
    go = lambda v, pairs: lax.ppermute(
        v, "col", [(i * cores + c, j * cores + c) for i, j in pairs for c in range(cores)]
    )
    if depth == 4:
        across = go(slab, [(i, i ^ 2) for i in range(4)])
        climbed = go(slab, [(i, i + 1) for i in range(3)])
        dropped = go(slab, [(i + 1, i) for i in range(3)])
        ends = go(across, [(1, 0), (2, 3)])
        turned = [climbed, across, dropped, ends]
    else:
        turned = [go(slab, [(i, (i + k) % depth) for i in range(depth)]) for k in range(1, depth)]

    wt = weight.T
    cut = round(local / 2 / LANES) * LANES
    last = cut + up(local - cut, LANES)
    edges_y = [0, cut - 3 * LANES, cut]
    edges_x = [cut, last - 4 * LANES, local]
    spans = list(zip(zip(edges_y, edges_y[1:]), zip(edges_x, edges_x[1:])))
    from_y, from_x = move(wt, 1, 0), {0: wt}
    for dx in range(1, nx):
        from_x[dx] = move(from_x[dx - 1], 0, 1)

    (*payloads, inf_blocks), turned = lax.optimization_barrier(((*payloads, inf_blocks), turned))
    arrived = [move(v, *o) for v, o in zip(payloads[1:-1], order[1:-1])]

    if depth == 4:
        climbed, across, dropped, ends = turned
        turned = [jnp.where(here == 0, ends, climbed), across, jnp.where(here == 3, ends, dropped)]
    acts_mine = jnp.stack([slab, *turned])
    core_at = core.reshape(1)
    acts_all = (acts_mine, lax.ppermute(acts_mine, "col", other_core))
    low = low_terms(core_at, acts_all, inf_blocks, tok, rank)
    onf = output_noise_factor.reshape(factors_here, local)
    onf = jnp.concatenate([onf] * 3, axis=0)
    acc = own_sum(place(0, 0), acts_all, wt, low, onf)
    payloads[-1], acc = lax.optimization_barrier((payloads[-1], acc))
    arrived.append(move(payloads[-1], *order[-1]))

    along_x = [from_x[dx] for dx in range(1, nx)]
    to_y = [[v[lo:hi] for v in along_x] for (lo, hi), _ in spans]
    to_x = [from_y[lo:hi] for _, (lo, hi) in spans]

    def relay(firsts, run):
        firsts, seconds = [move(v, 1, 0) for v in firsts], []
        for dx in range(1, nx):
            run = move(run, 0, 1)
            seconds.append(run)
        return firsts, seconds

    lasts = [relay(to_y[0], to_x[0])]
    near = [place(0, dx) for dx in range(1, nx)] + [place(1, 0)]
    acc = near_sum(near, acts_all, acc, [*along_x, from_y])

    arrived, acc = lax.optimization_barrier((arrived, acc))
    factors = jnp.concatenate([payloads[0], *arrived], axis=0)
    sums = sum_squares(factors, wide, local)
    reach = 1
    while reach < cols:
        sums = sums + lax.ppermute(sums, "col", [(i, i ^ reach) for i in range(cols)])
        reach *= 2
    everywhere = [move(sums, *o) for o in order[1:]]
    to_y[1], to_x[1], everywhere = lax.optimization_barrier((to_y[1], to_x[1], everywhere))
    lasts.append(relay(to_y[1], to_x[1]))
    sums = sum(everywhere, sums)
    step_dir, new_weight = apply_step(sums, factors, wide, wt, width * local * cols)

    out = None
    blocks = [place(1, dx) for dx in range(1, nx)]
    for ((lo, hi), (also_lo, also_hi)), (firsts, seconds) in zip(spans, lasts):
        bn = next(n for n in (384, LANES) if lo % n == hi % n == also_lo % n == 0)
        at = [*range(lo // bn, hi // bn), *range(also_lo // bn, pl.cdiv(also_hi, bn))]
        out = far_sum(core_at, at, blocks, acts_all, acc, firsts, seconds, out, bn)
    return out.reshape(members, tok, local), step_dir.T, new_weight.T


def solution(mesh):
    in_specs = (
        P("pop", None, "col"),
        P("pop", "col"),
        P("pop", None, None),
        P("pop", None, "col"),
        P("pop"),
    )
    out_specs = (P("pop", None, "col"), P("pop", "col"), P("pop", "col"))
    return jax.shard_map(body, mesh=mesh, in_specs=in_specs, out_specs=out_specs, check_vma=False)
```

```python
import functools

import jax
import jax.numpy as jnp
from jax import lax
from jax.experimental import pallas as pl
from jax.experimental.pallas import tpu as pltpu
from jax.sharding import PartitionSpec as P

VMEM = 36 * 1024 * 1024
LANES = 128
NT = (((1,), (1,)), ((), ()))
TN = (((0,), (0,)), ((), ()))


def up(n, m):
    return -(-n // m) * m


def call(kernel, vmem=VMEM, **kw):
    return pl.pallas_call(
        kernel,
        compiler_params=pltpu.CompilerParams(vmem_limit_bytes=vmem),
        cost_estimate=pl.CostEstimate(flops=1, bytes_accessed=1, transcendentals=0),
        **kw,
    )


def low_kernel(core_ref, mine_ref, theirs_ref, inf_ref, out_ref, acc_ref, *, tok, rank):
    k = pl.program_id(0)

    @pl.when(k == 0)
    def _():
        acc_ref[...] = jnp.zeros_like(acc_ref)

    for s, acts in enumerate((mine_ref, theirs_ref)):
        acc_ref[s] += lax.dot_general(acts[...], inf_ref[...], NT, preferred_element_type=jnp.float32)

    @pl.when(k == pl.num_programs(0) - 1)
    def _():
        for s in range(2):
            full = acc_ref[s]
            rows, n = full.shape
            base = (core_ref[0] ^ s) * rows
            row = (base + lax.broadcasted_iota(jnp.int32, full.shape, 0)) // tok
            col = lax.broadcasted_iota(jnp.int32, full.shape, 1) // rank
            rest = jnp.where(row == col, 0.5 * full, 0.0)
            for i in range(3):
                part = rest.astype(jnp.bfloat16)
                out_ref[s, :, i * n : (i + 1) * n] = part
                rest = rest - part.astype(jnp.float32)


def low_terms(core, acts, inf, tok, rank):
    blocks, rows, kb = acts[0].shape
    n = inf.shape[1]
    act = pl.BlockSpec((None, rows, kb), lambda k, _: (k, 0, 0))
    return call(
        functools.partial(low_kernel, tok=tok, rank=rank),
        grid_spec=pltpu.PrefetchScalarGridSpec(
            num_scalar_prefetch=1,
            grid=(blocks,),
            in_specs=[act, act, pl.BlockSpec((None, n, kb), lambda k, _: (k, 0, 0))],
            out_specs=pl.BlockSpec((2, rows, 3 * n), lambda k, _: (0, 0, 0)),
            scratch_shapes=[pltpu.VMEM((2, rows, n), jnp.float32)],
        ),
        out_shape=jax.ShapeDtypeStruct((2, rows, 3 * n), jnp.bfloat16),
    )(core, *acts, inf)


def own_kernel(idx_ref, mine_ref, theirs_ref, weight_ref, low_ref, onf_ref, out_ref):
    del idx_ref
    for s, acts in enumerate((mine_ref, theirs_ref)):
        total = jnp.dot(low_ref[s], onf_ref[...], preferred_element_type=jnp.float32)
        out_ref[s] = total + lax.dot_general(
            acts[...], weight_ref[...], NT, preferred_element_type=jnp.float32
        )


def own_sum(block, acts, weight, low, onf, bn=512):
    _, rows, kb = acts[0].shape
    cols = weight.shape[0]
    act = pl.BlockSpec((None, rows, kb), lambda n, ref: (ref[0], 0, 0))
    return call(
        own_kernel,
        grid_spec=pltpu.PrefetchScalarGridSpec(
            num_scalar_prefetch=1,
            grid=(pl.cdiv(cols, bn),),
            in_specs=[
                act,
                act,
                pl.BlockSpec((bn, kb), lambda n, _: (n, 0)),
                pl.BlockSpec(low.shape, lambda n, _: (0, 0, 0)),
                pl.BlockSpec((onf.shape[0], bn), lambda n, _: (0, n)),
            ],
            out_specs=pl.BlockSpec((2, rows, bn), lambda n, _: (0, 0, n)),
        ),
        out_shape=jax.ShapeDtypeStruct((2, rows, cols), jnp.float32),
    )(block.reshape(1), *acts, weight, low, onf)


def near_kernel(idx_ref, acc_ref, *refs, count):
    del idx_ref
    acts, weights, out_ref = refs[: 2 * count], refs[2 * count : 3 * count], refs[-1]
    for s in range(2):
        total = acc_ref[s]
        for i, w in enumerate(weights):
            total += lax.dot_general(
                acts[2 * i + s][...], w[...], NT, preferred_element_type=jnp.float32
            )
        out_ref[s] = total


def near_sum(blocks, acts, acc, weights, bn=512):
    _, rows, kb = acts[0].shape
    cols = weights[0].shape[0]
    count = len(weights)
    specs = [pl.BlockSpec((2, rows, bn), lambda n, _: (0, 0, n))]
    args = []
    for i in range(count):
        act = pl.BlockSpec(
            (None, rows, kb), functools.partial(lambda n, ref, i: (ref[i], 0, 0), i=i)
        )
        specs += [act, act]
        args += list(acts)
    specs += [pl.BlockSpec((bn, kb), lambda n, _: (n, 0))] * count
    return call(
        functools.partial(near_kernel, count=count),
        vmem=40 * 1024 * 1024,
        grid_spec=pltpu.PrefetchScalarGridSpec(
            num_scalar_prefetch=1,
            grid=(pl.cdiv(cols, bn),),
            in_specs=specs,
            out_specs=pl.BlockSpec((2, rows, bn), lambda n, _: (0, 0, n)),
        ),
        out_shape=jax.ShapeDtypeStruct((2, rows, cols), jnp.float32),
    )(jnp.stack(blocks), acc, *args, *weights)


def far_kernel(at_ref, idx_ref, acc_ref, *refs, count, split):
    del at_ref
    acts, firsts = refs[: 2 * count], refs[2 * count : 3 * count]
    seconds, out_ref = refs[3 * count : 4 * count], refs[-1]
    rows = acc_ref.shape[1]

    def run(weights):
        for s in range(2):
            total = acc_ref[s]
            for i, w in enumerate(weights):
                total += lax.dot_general(
                    acts[2 * i + s][...], w[...], NT, preferred_element_type=jnp.float32
                )
            at = pl.multiple_of((idx_ref[0] ^ s) * rows, rows)
            out_ref[pl.ds(at, rows), :] = total.astype(out_ref.dtype)

    pl.when(pl.program_id(0) < split)(lambda: run(firsts))
    pl.when(pl.program_id(0) >= split)(lambda: run(seconds))


def far_sum(core, at, blocks, acts, acc, firsts, seconds, out, bn):
    _, rows, kb = acts[0].shape
    cols = acc.shape[2]
    count = len(firsts)
    split = firsts[0].shape[0] // bn
    specs = [pl.BlockSpec((2, rows, bn), lambda n, at, _: (0, 0, at[n]))]
    args = []
    for i in range(count):
        act = pl.BlockSpec(
            (None, rows, kb), functools.partial(lambda n, at, ref, i: (ref[i], 0, 0), i=i + 1)
        )
        specs += [act, act]
        args += list(acts)
    specs += [pl.BlockSpec((bn, kb), lambda n, at, _: (jnp.minimum(n, split - 1), 0))] * count
    specs += [pl.BlockSpec((bn, kb), lambda n, at, _: (jnp.maximum(n - split, 0), 0))] * count
    args += firsts + seconds
    alias = {}
    if out is not None:
        specs.append(pl.BlockSpec(memory_space=pl.ANY))
        args.append(out)
        alias = {len(args) + 2: 0}
    return call(
        functools.partial(far_kernel, count=count, split=split),
        vmem=56 * 1024 * 1024,
        grid_spec=pltpu.PrefetchScalarGridSpec(
            num_scalar_prefetch=2,
            grid=(len(at),),
            in_specs=specs,
            out_specs=pl.BlockSpec((2 * rows, bn), lambda n, at, _: (0, at[n])),
        ),
        out_shape=jax.ShapeDtypeStruct((2 * rows, cols), jnp.bfloat16),
        input_output_aliases=alias,
    )(jnp.array(at, jnp.int32), jnp.concatenate([core, jnp.stack(blocks)]), acc, *args)


def square_kernel(left_ref, right_ref, out_ref, *, cols):
    n = pl.program_id(0)
    delta = lax.dot_general(
        right_ref[...], left_ref[...], TN, preferred_element_type=jnp.float32
    )
    at = n * delta.shape[0] + lax.broadcasted_iota(jnp.int32, delta.shape, 0)
    delta = jnp.where(at < cols, delta, 0.0)

    @pl.when(n == 0)
    def _():
        out_ref[...] = jnp.zeros_like(out_ref)

    part = jnp.sum((delta * delta).reshape(-1, 8, delta.shape[1]), axis=0)
    for j in range(0, delta.shape[1], LANES):
        out_ref[...] += part[:, j : j + LANES]


def sum_squares(factors, wide, cols):
    k = factors.shape[0]
    return call(
        functools.partial(square_kernel, cols=cols),
        grid=(pl.cdiv(cols, wide),),
        in_specs=[
            pl.BlockSpec((k, wide), lambda n: (0, 0)),
            pl.BlockSpec((k, wide), lambda n: (0, n + 1)),
        ],
        out_specs=pl.BlockSpec((8, LANES), lambda n: (0, 0)),
        out_shape=jax.ShapeDtypeStruct((8, LANES), jnp.float32),
    )(factors, factors)


def step_kernel(sums_ref, left_ref, right_ref, weight_ref, step_ref, new_ref, *, count):
    mean_sq = jnp.sum(sums_ref[...]) / count
    scale = lax.rsqrt(jnp.full((1, 1), mean_sq + 1e-06, jnp.float32))
    delta = lax.dot_general(
        right_ref[...], left_ref[...], TN, preferred_element_type=jnp.float32
    )
    step = delta[:, : step_ref.shape[1]] * scale
    step_ref[...] = step
    new_ref[...] = (weight_ref[...].astype(jnp.float32) + 0.01 * step).astype(new_ref.dtype)


def apply_step(sums, factors, wide, weight, count):
    cols, rows = weight.shape
    k = factors.shape[0]
    block = pl.BlockSpec((wide, rows), lambda n: (n, 0))
    return call(
        functools.partial(step_kernel, count=count),
        grid=(pl.cdiv(cols, wide),),
        in_specs=[
            pl.BlockSpec(sums.shape, lambda n: (0, 0)),
            pl.BlockSpec((k, wide), lambda n: (0, 0)),
            pl.BlockSpec((k, wide), lambda n: (0, n + 1)),
            block,
        ],
        out_specs=[block, block],
        out_shape=[
            jax.ShapeDtypeStruct((cols, rows), jnp.float32),
            jax.ShapeDtypeStruct((cols, rows), weight.dtype),
        ],
    )(sums, factors, factors, weight)


def body(acts, weight, input_noise_factor, output_noise_factor, ranks):
    members, tok, kb = acts.shape
    rank, width = input_noise_factor.shape[1:]
    pops, cols = lax.axis_size("pop"), lax.axis_size("col")
    ny, cores = 2, 2
    nx = pops // ny
    total_members = members * pops
    local = output_noise_factor.shape[2]
    rows = width // pops
    factors_here = members * rank
    pop = lax.axis_index("pop").astype(jnp.int32)
    core = lax.rem(lax.axis_index("col").astype(jnp.int32), cores)
    y, x = pop // nx, lax.rem(pop, nx)

    def place(dy, dx):
        source = lax.rem(y + dy, ny) * nx + lax.rem(x + nx - dx, nx)
        return lax.rem(lax.axis_index("col").astype(jnp.int32) // cores + pops - source, pops)

    def move(v, dy, dx):
        route = [(i, (i // nx + dy) % ny * nx + (i + dx) % nx) for i in range(pops)]
        return lax.ppermute(v, "pop", route)

    other_core = [(i, i ^ 1) for i in range(cols)]

    wide = up(rows, LANES)
    fit = ranks.astype(jnp.float32) / (total_members - 1) - 0.5
    scaled = (output_noise_factor.astype(jnp.float32) * fit[:, None, None]).astype(jnp.bfloat16)
    scaled = scaled.reshape(factors_here, local)
    inf = input_noise_factor.reshape(factors_here, width)

    def rows_for(dy, dx):
        target = lax.rem(y + dy, ny) * nx + lax.rem(x + dx, nx)
        part = lax.dynamic_slice_in_dim(inf, target * rows, rows, axis=1)
        return jnp.pad(part, ((0, 0), (0, wide - rows)))

    join = lambda *parts: jnp.concatenate(parts, axis=1)
    order = [(dy, dx) for dy in range(ny) for dx in range(nx)]
    payloads = [join(rows_for(*o), scaled) for o in order]

    flat = acts.reshape(members * tok, kb)
    half = members * tok // cores
    mine = lax.dynamic_slice_in_dim(flat, core * half, half, axis=0)
    theirs = lax.dynamic_slice_in_dim(flat, (1 - core) * half, half, axis=0)
    theirs = lax.ppermute(theirs, "col", other_core)
    slab = jnp.where(core == 0, join(mine, theirs), join(theirs, mine))
    depth = cols // cores
    assert depth == pops
    here = lax.axis_index("col").astype(jnp.int32) // cores
    inf_blocks = inf.reshape(factors_here, pops, rows).transpose(1, 0, 2)
    inf_blocks = inf_blocks[lax.rem(here + pops - jnp.arange(pops, dtype=jnp.int32), pops)]
    go = lambda v, pairs: lax.ppermute(
        v, "col", [(i * cores + c, j * cores + c) for i, j in pairs for c in range(cores)]
    )
    if depth == 4:
        across = go(slab, [(i, i ^ 2) for i in range(4)])
        climbed = go(slab, [(i, i + 1) for i in range(3)])
        dropped = go(slab, [(i + 1, i) for i in range(3)])
        ends = go(across, [(1, 0), (2, 3)])
        turned = [climbed, across, dropped, ends]
        swapped = [lax.ppermute(v, "col", other_core) for v in [slab, *turned]]
    else:
        turned = [go(slab, [(i, (i + k) % depth) for i in range(depth)]) for k in range(1, depth)]

    wt = weight.T
    cut = round(local / 2 / LANES) * LANES
    last = cut + up(local - cut, LANES)
    edges_y = [0, cut - 3 * LANES, cut]
    edges_x = [cut, last - 4 * LANES, local]
    spans = list(zip(zip(edges_y, edges_y[1:]), zip(edges_x, edges_x[1:])))
    from_y, from_x = move(wt, 1, 0), {0: wt}
    for dx in range(1, nx):
        from_x[dx] = move(from_x[dx - 1], 0, 1)

    (*payloads, inf_blocks), turned = lax.optimization_barrier(((*payloads, inf_blocks), turned))
    arrived = [move(v, *o) for v, o in zip(payloads[1:-1], order[1:-1])]

    def gathered(slab, climbed, across, dropped, ends):
        parts = [jnp.where(here == 0, ends, climbed), across, jnp.where(here == 3, ends, dropped)]
        return jnp.stack([slab, *parts])

    acts_mine = gathered(slab, *turned) if depth == 4 else jnp.stack([slab, *turned])
    core_at = core.reshape(1)
    acts_theirs = gathered(*swapped) if depth == 4 else lax.ppermute(acts_mine, "col", other_core)
    acts_all = (acts_mine, acts_theirs)
    low = low_terms(core_at, acts_all, inf_blocks, tok, rank)
    onf = output_noise_factor.reshape(factors_here, local)
    onf = jnp.concatenate([onf] * 3, axis=0)
    acc = own_sum(place(0, 0), acts_all, wt, low, onf)
    payloads[-1], acc, from_x, from_y = lax.optimization_barrier((payloads[-1], acc, from_x, from_y))
    arrived.append(move(payloads[-1], *order[-1]))

    along_x = [from_x[dx] for dx in range(1, nx)]
    to_y = [[v[lo:hi] for v in along_x] for (lo, hi), _ in spans]
    to_x = [from_y[lo:hi] for _, (lo, hi) in spans]

    def relay(firsts, run):
        firsts, seconds = [move(v, 1, 0) for v in firsts], []
        for dx in range(1, nx):
            run = move(run, 0, 1)
            seconds.append(run)
        return firsts, seconds

    lasts = [relay(to_y[0], to_x[0])]
    near = [place(0, dx) for dx in range(1, nx)] + [place(1, 0)]
    acc = near_sum(near, acts_all, acc, [*along_x, from_y])

    arrived, acc = lax.optimization_barrier((arrived, acc))
    factors = jnp.concatenate([payloads[0], *arrived], axis=0)
    sums = sum_squares(factors, wide, local)
    reach = 1
    while reach < cols:
        sums = sums + lax.ppermute(sums, "col", [(i, i ^ reach) for i in range(cols)])
        reach *= 2
    everywhere = [move(sums, *o) for o in order[1:]]
    to_y[1], to_x[1], everywhere = lax.optimization_barrier((to_y[1], to_x[1], everywhere))
    lasts.append(relay(to_y[1], to_x[1]))
    sums = sum(everywhere, sums)
    step_dir, new_weight = apply_step(sums, factors, wide, wt, width * local * cols)

    out = None
    blocks = [place(1, dx) for dx in range(1, nx)]
    for ((lo, hi), (also_lo, also_hi)), (firsts, seconds) in zip(spans, lasts):
        bn = next(n for n in (384, LANES) if lo % n == hi % n == also_lo % n == 0)
        at = [*range(lo // bn, hi // bn), *range(also_lo // bn, pl.cdiv(also_hi, bn))]
        out = far_sum(core_at, at, blocks, acts_all, acc, firsts, seconds, out, bn)
    return out.reshape(members, tok, local), step_dir.T, new_weight.T


def solution(mesh):
    in_specs = (
        P("pop", None, "col"),
        P("pop", "col"),
        P("pop", None, None),
        P("pop", None, "col"),
        P("pop"),
    )
    out_specs = (P("pop", None, "col"), P("pop", "col"), P("pop", "col"))
    return jax.shard_map(body, mesh=mesh, in_specs=in_specs, out_specs=out_specs, check_vma=False)
```

```python
import functools

import jax
import jax.numpy as jnp
from jax import lax
from jax.experimental import pallas as pl
from jax.experimental.pallas import tpu as pltpu
from jax.sharding import PartitionSpec as P

VMEM = 36 * 1024 * 1024
LANES = 128
NT = (((1,), (1,)), ((), ()))
TN = (((0,), (0,)), ((), ()))


def up(n, m):
    return -(-n // m) * m


def call(kernel, vmem=VMEM, **kw):
    return pl.pallas_call(
        kernel,
        compiler_params=pltpu.CompilerParams(vmem_limit_bytes=vmem),
        cost_estimate=pl.CostEstimate(flops=1, bytes_accessed=1, transcendentals=0),
        **kw,
    )


def low_kernel(core_ref, mine_ref, theirs_ref, inf_ref, out_ref, acc_ref, *, tok, rank):
    k = pl.program_id(0)

    @pl.when(k == 0)
    def _():
        acc_ref[...] = jnp.zeros_like(acc_ref)

    for s, acts in enumerate((mine_ref, theirs_ref)):
        acc_ref[s] += lax.dot_general(acts[...], inf_ref[...], NT, preferred_element_type=jnp.float32)

    @pl.when(k == pl.num_programs(0) - 1)
    def _():
        for s in range(2):
            full = acc_ref[s]
            rows, n = full.shape
            base = (core_ref[0] ^ s) * rows
            row = (base + lax.broadcasted_iota(jnp.int32, full.shape, 0)) // tok
            col = lax.broadcasted_iota(jnp.int32, full.shape, 1) // rank
            rest = jnp.where(row == col, 0.5 * full, 0.0)
            for i in range(3):
                part = rest.astype(jnp.bfloat16)
                out_ref[s, :, i * n : (i + 1) * n] = part
                rest = rest - part.astype(jnp.float32)


def low_terms(core, acts, inf, tok, rank):
    blocks, rows, kb = acts[0].shape
    n = inf.shape[1]
    act = pl.BlockSpec((None, rows, kb), lambda k, _: (k, 0, 0))
    return call(
        functools.partial(low_kernel, tok=tok, rank=rank),
        grid_spec=pltpu.PrefetchScalarGridSpec(
            num_scalar_prefetch=1,
            grid=(blocks,),
            in_specs=[act, act, pl.BlockSpec((None, n, kb), lambda k, _: (k, 0, 0))],
            out_specs=pl.BlockSpec((2, rows, 3 * n), lambda k, _: (0, 0, 0)),
            scratch_shapes=[pltpu.VMEM((2, rows, n), jnp.float32)],
        ),
        out_shape=jax.ShapeDtypeStruct((2, rows, 3 * n), jnp.bfloat16),
    )(core, *acts, inf)


def own_kernel(idx_ref, mine_ref, theirs_ref, weight_ref, low_ref, onf_ref, out_ref):
    del idx_ref
    for s, acts in enumerate((mine_ref, theirs_ref)):
        total = jnp.dot(low_ref[s], onf_ref[...], preferred_element_type=jnp.float32)
        out_ref[s] = total + lax.dot_general(
            acts[...], weight_ref[...], NT, preferred_element_type=jnp.float32
        )


def own_sum(block, acts, weight, low, onf, bn=512):
    _, rows, kb = acts[0].shape
    cols = weight.shape[0]
    act = pl.BlockSpec((None, rows, kb), lambda n, ref: (ref[0], 0, 0))
    return call(
        own_kernel,
        grid_spec=pltpu.PrefetchScalarGridSpec(
            num_scalar_prefetch=1,
            grid=(pl.cdiv(cols, bn),),
            in_specs=[
                act,
                act,
                pl.BlockSpec((bn, kb), lambda n, _: (n, 0)),
                pl.BlockSpec(low.shape, lambda n, _: (0, 0, 0)),
                pl.BlockSpec((onf.shape[0], bn), lambda n, _: (0, n)),
            ],
            out_specs=pl.BlockSpec((2, rows, bn), lambda n, _: (0, 0, n)),
        ),
        out_shape=jax.ShapeDtypeStruct((2, rows, cols), jnp.float32),
    )(block.reshape(1), *acts, weight, low, onf)


def near_kernel(idx_ref, acc_ref, *refs, count):
    del idx_ref
    acts, weights, out_ref = refs[: 2 * count], refs[2 * count : 3 * count], refs[-1]
    for s in range(2):
        total = acc_ref[s]
        for i, w in enumerate(weights):
            total += lax.dot_general(
                acts[2 * i + s][...], w[...], NT, preferred_element_type=jnp.float32
            )
        out_ref[s] = total


def near_sum(blocks, acts, acc, weights, bn=512):
    _, rows, kb = acts[0].shape
    cols = weights[0].shape[0]
    count = len(weights)
    specs = [pl.BlockSpec((2, rows, bn), lambda n, _: (0, 0, n))]
    args = []
    for i in range(count):
        act = pl.BlockSpec(
            (None, rows, kb), functools.partial(lambda n, ref, i: (ref[i], 0, 0), i=i)
        )
        specs += [act, act]
        args += list(acts)
    specs += [pl.BlockSpec((bn, kb), lambda n, _: (n, 0))] * count
    return call(
        functools.partial(near_kernel, count=count),
        vmem=40 * 1024 * 1024,
        grid_spec=pltpu.PrefetchScalarGridSpec(
            num_scalar_prefetch=1,
            grid=(pl.cdiv(cols, bn),),
            in_specs=specs,
            out_specs=pl.BlockSpec((2, rows, bn), lambda n, _: (0, 0, n)),
        ),
        out_shape=jax.ShapeDtypeStruct((2, rows, cols), jnp.float32),
    )(jnp.stack(blocks), acc, *args, *weights)


def far_kernel(at_ref, idx_ref, acc_ref, *refs, count, split):
    del at_ref
    acts, firsts = refs[: 2 * count], refs[2 * count : 3 * count]
    seconds, out_ref = refs[3 * count : 4 * count], refs[-1]
    rows = acc_ref.shape[1]

    def run(weights):
        for s in range(2):
            total = acc_ref[s]
            for i, w in enumerate(weights):
                total += lax.dot_general(
                    acts[2 * i + s][...], w[...], NT, preferred_element_type=jnp.float32
                )
            at = pl.multiple_of((idx_ref[0] ^ s) * rows, rows)
            out_ref[pl.ds(at, rows), :] = total.astype(out_ref.dtype)

    pl.when(pl.program_id(0) < split)(lambda: run(firsts))
    pl.when(pl.program_id(0) >= split)(lambda: run(seconds))


def far_sum(core, at, blocks, acts, acc, firsts, seconds, out, bn):
    _, rows, kb = acts[0].shape
    cols = acc.shape[2]
    count = len(firsts)
    split = firsts[0].shape[0] // bn
    specs = [pl.BlockSpec((2, rows, bn), lambda n, at, _: (0, 0, at[n]))]
    args = []
    for i in range(count):
        act = pl.BlockSpec(
            (None, rows, kb), functools.partial(lambda n, at, ref, i: (ref[i], 0, 0), i=i + 1)
        )
        specs += [act, act]
        args += list(acts)
    specs += [pl.BlockSpec((bn, kb), lambda n, at, _: (jnp.minimum(n, split - 1), 0))] * count
    specs += [pl.BlockSpec((bn, kb), lambda n, at, _: (jnp.maximum(n - split, 0), 0))] * count
    args += firsts + seconds
    alias = {}
    if out is not None:
        specs.append(pl.BlockSpec(memory_space=pl.ANY))
        args.append(out)
        alias = {len(args) + 2: 0}
    return call(
        functools.partial(far_kernel, count=count, split=split),
        vmem=56 * 1024 * 1024,
        grid_spec=pltpu.PrefetchScalarGridSpec(
            num_scalar_prefetch=2,
            grid=(len(at),),
            in_specs=specs,
            out_specs=pl.BlockSpec((2 * rows, bn), lambda n, at, _: (0, at[n])),
        ),
        out_shape=jax.ShapeDtypeStruct((2 * rows, cols), jnp.bfloat16),
        input_output_aliases=alias,
    )(jnp.array(at, jnp.int32), jnp.concatenate([core, jnp.stack(blocks)]), acc, *args)


def square_kernel(left_ref, right_ref, out_ref, *, cols):
    n = pl.program_id(0)
    delta = lax.dot_general(
        right_ref[...], left_ref[...], TN, preferred_element_type=jnp.float32
    )
    at = n * delta.shape[0] + lax.broadcasted_iota(jnp.int32, delta.shape, 0)
    delta = jnp.where(at < cols, delta, 0.0)

    @pl.when(n == 0)
    def _():
        out_ref[...] = jnp.zeros_like(out_ref)

    part = jnp.sum((delta * delta).reshape(-1, 8, delta.shape[1]), axis=0)
    for j in range(0, delta.shape[1], LANES):
        out_ref[...] += part[:, j : j + LANES]


def sum_squares(factors, wide, cols):
    k = factors.shape[0]
    return call(
        functools.partial(square_kernel, cols=cols),
        grid=(pl.cdiv(cols, wide),),
        in_specs=[
            pl.BlockSpec((k, wide), lambda n: (0, 0)),
            pl.BlockSpec((k, wide), lambda n: (0, n + 1)),
        ],
        out_specs=pl.BlockSpec((8, LANES), lambda n: (0, 0)),
        out_shape=jax.ShapeDtypeStruct((8, LANES), jnp.float32),
    )(factors, factors)


def step_kernel(sums_ref, left_ref, right_ref, weight_ref, step_ref, new_ref, *, count):
    mean_sq = jnp.sum(sums_ref[...]) / count
    scale = lax.rsqrt(jnp.full((1, 1), mean_sq + 1e-06, jnp.float32))
    delta = lax.dot_general(
        right_ref[...], left_ref[...], TN, preferred_element_type=jnp.float32
    )
    step = delta[:, : step_ref.shape[1]] * scale
    step_ref[...] = step
    new_ref[...] = (weight_ref[...].astype(jnp.float32) + 0.01 * step).astype(new_ref.dtype)


def apply_step(sums, factors, wide, weight, count):
    cols, rows = weight.shape
    k = factors.shape[0]
    block = pl.BlockSpec((wide, rows), lambda n: (n, 0))
    return call(
        functools.partial(step_kernel, count=count),
        grid=(pl.cdiv(cols, wide),),
        in_specs=[
            pl.BlockSpec(sums.shape, lambda n: (0, 0)),
            pl.BlockSpec((k, wide), lambda n: (0, 0)),
            pl.BlockSpec((k, wide), lambda n: (0, n + 1)),
            block,
        ],
        out_specs=[block, block],
        out_shape=[
            jax.ShapeDtypeStruct((cols, rows), jnp.float32),
            jax.ShapeDtypeStruct((cols, rows), weight.dtype),
        ],
    )(sums, factors, factors, weight)


def body(acts, weight, input_noise_factor, output_noise_factor, ranks):
    members, tok, kb = acts.shape
    rank, width = input_noise_factor.shape[1:]
    pops, cols = lax.axis_size("pop"), lax.axis_size("col")
    ny, cores = 2, 2
    nx = pops // ny
    total_members = members * pops
    local = output_noise_factor.shape[2]
    rows = width // pops
    factors_here = members * rank
    pop = lax.axis_index("pop").astype(jnp.int32)
    core = lax.rem(lax.axis_index("col").astype(jnp.int32), cores)
    y, x = pop // nx, lax.rem(pop, nx)

    def place(dy, dx):
        source = lax.rem(y + dy, ny) * nx + lax.rem(x + nx - dx, nx)
        return lax.rem(lax.axis_index("col").astype(jnp.int32) // cores + pops - source, pops)

    def move(v, dy, dx):
        route = [(i, (i // nx + dy) % ny * nx + (i + dx) % nx) for i in range(pops)]
        return lax.ppermute(v, "pop", route)

    other_core = [(i, i ^ 1) for i in range(cols)]

    wide = up(rows, LANES)
    fit = ranks.astype(jnp.float32) / (total_members - 1) - 0.5
    scaled = (output_noise_factor.astype(jnp.float32) * fit[:, None, None]).astype(jnp.bfloat16)
    scaled = scaled.reshape(factors_here, local)
    inf = input_noise_factor.reshape(factors_here, width)

    def rows_for(dy, dx):
        target = lax.rem(y + dy, ny) * nx + lax.rem(x + dx, nx)
        part = lax.dynamic_slice_in_dim(inf, target * rows, rows, axis=1)
        return jnp.pad(part, ((0, 0), (0, wide - rows)))

    join = lambda *parts: jnp.concatenate(parts, axis=1)
    order = [(dy, dx) for dy in range(ny) for dx in range(nx)]
    payloads = [join(rows_for(*o), scaled) for o in order]

    flat = acts.reshape(members * tok, kb)
    half = members * tok // cores
    mine = lax.dynamic_slice_in_dim(flat, core * half, half, axis=0)
    theirs = lax.dynamic_slice_in_dim(flat, (1 - core) * half, half, axis=0)
    theirs = lax.ppermute(theirs, "col", other_core)
    slab = jnp.where(core == 0, join(mine, theirs), join(theirs, mine))
    depth = cols // cores
    assert depth == pops
    here = lax.axis_index("col").astype(jnp.int32) // cores
    inf_blocks = inf.reshape(factors_here, pops, rows).transpose(1, 0, 2)
    inf_blocks = inf_blocks[lax.rem(here + pops - jnp.arange(pops, dtype=jnp.int32), pops)]
    go = lambda v, pairs: lax.ppermute(
        v, "col", [(i * cores + c, j * cores + c) for i, j in pairs for c in range(cores)]
    )
    if depth == 4:
        across = go(slab, [(i, i ^ 2) for i in range(4)])
        climbed = go(slab, [(i, i + 1) for i in range(3)])
        dropped = go(slab, [(i + 1, i) for i in range(3)])
        ends = go(across, [(1, 0), (2, 3)])
        turned = [climbed, across, dropped, ends]
        swapped = [lax.ppermute(v, "col", other_core) for v in [slab, *turned]]
    else:
        turned = [go(slab, [(i, (i + k) % depth) for i in range(depth)]) for k in range(1, depth)]

    wt = weight.T
    cut = round(local / 2 / LANES) * LANES
    last = cut + up(local - cut, LANES)
    edges_y = [0, cut - 3 * LANES, cut]
    edges_x = [cut, last - 4 * LANES, local]
    spans = list(zip(zip(edges_y, edges_y[1:]), zip(edges_x, edges_x[1:])))
    from_y, from_x = move(wt, 1, 0), {0: wt}
    for dx in range(1, nx):
        from_x[dx] = move(from_x[dx - 1], 0, 1)

    (*payloads, inf_blocks), turned = lax.optimization_barrier(((*payloads, inf_blocks), turned))
    arrived = [move(v, *o) for v, o in zip(payloads[1:-1], order[1:-1])]

    def gathered(slab, climbed, across, dropped, ends):
        parts = [jnp.where(here == 0, ends, climbed), across, jnp.where(here == 3, ends, dropped)]
        return jnp.stack([slab, *parts])

    acts_mine = gathered(slab, *turned) if depth == 4 else jnp.stack([slab, *turned])
    core_at = core.reshape(1)
    acts_theirs = gathered(*swapped) if depth == 4 else lax.ppermute(acts_mine, "col", other_core)
    acts_all = (acts_mine, acts_theirs)
    low = low_terms(core_at, acts_all, inf_blocks, tok, rank)
    onf = output_noise_factor.reshape(factors_here, local)
    onf = jnp.concatenate([onf] * 3, axis=0)
    acc = own_sum(place(0, 0), acts_all, wt, low, onf)
    payloads[-1], acc, from_x, from_y = lax.optimization_barrier((payloads[-1], acc, from_x, from_y))
    arrived.append(move(payloads[-1], *order[-1]))

    along_x = [from_x[dx] for dx in range(1, nx)]
    to_y = [[v[lo:hi] for v in along_x] for (lo, hi), _ in spans]
    to_x = [from_y[lo:hi] for _, (lo, hi) in spans]

    def relay(firsts, run):
        firsts, seconds = [move(v, 1, 0) for v in firsts], []
        for dx in range(1, nx):
            run = move(run, 0, 1)
            seconds.append(run)
        return firsts, seconds

    lasts = [relay(to_y[0], to_x[0])]
    near = [place(0, dx) for dx in range(1, nx)] + [place(1, 0)]
    acc = near_sum(near, acts_all, acc, [*along_x, from_y])

    arrived, acc = lax.optimization_barrier((arrived, acc))
    factors = jnp.concatenate([payloads[0], *arrived], axis=0)
    sums = sum_squares(factors, wide, local)
    reach = 1
    while reach < cols:
        sums = sums + lax.ppermute(sums, "col", [(i, i ^ reach) for i in range(cols)])
        reach *= 2
    everywhere = [move(sums, *o) for o in order[1:]]
    to_y[1], to_x[1], everywhere = lax.optimization_barrier((to_y[1], to_x[1], everywhere))
    lasts.append(relay(to_y[1], to_x[1]))
    sums = sum(everywhere, sums)
    out = None
    blocks = [place(1, dx) for dx in range(1, nx)]
    for ((lo, hi), (also_lo, also_hi)), (firsts, seconds) in zip(spans, lasts):
        bn = next(n for n in (384, LANES) if lo % n == hi % n == also_lo % n == 0)
        at = [*range(lo // bn, hi // bn), *range(also_lo // bn, pl.cdiv(also_hi, bn))]
        out = far_sum(core_at, at, blocks, acts_all, acc, firsts, seconds, out, bn)
        if (lo, hi) == spans[0][0]:
            sums, out = lax.optimization_barrier((sums, out))
            step_dir, new_weight = apply_step(sums, factors, wide, wt, width * local * cols)
    return out.reshape(members, tok, local), step_dir.T, new_weight.T


def solution(mesh):
    in_specs = (
        P("pop", None, "col"),
        P("pop", "col"),
        P("pop", None, None),
        P("pop", None, "col"),
        P("pop"),
    )
    out_specs = (P("pop", None, "col"), P("pop", "col"), P("pop", "col"))
    return jax.shard_map(body, mesh=mesh, in_specs=in_specs, out_specs=out_specs, check_vma=False)
```
